512 devices in a mesh: member: 16 (over y_hi, z), tile: 32 (over x, y_lo, core).
Axes of the slice: x: 4, y: 8 (y_hi: 2, y_lo: 4; y = y_hi * 4 + y_lo), z: 8, core: 2. Of those that a mesh axis runs over, the one named last changes fastest.
Arguments:
- anomalies: bfloat16 [16, 256, 2, 128, 128], P('member', 'tile'), may hold values from -6 to 6
- weights: bfloat16 [16, 256, 16], P('member', 'tile'), may hold values from -2 to 2
- diffusivity: float32 [256, 128, 128], P('tile'), may hold values from 0.05 to 1.2
- land_mask: int32 [256, 128, 128], P('tile'), may hold values 0 or 1
- neighbours: int32 [256, 4], P('tile'), may hold values from -1 to 255, as said below
Outputs:
- analysis_increment: bfloat16 [16, 256, 2, 128, 128], P('member', 'tile')
The draws below stay inside these ranges and needn't reach their ends.
Inputs may be any that keep to these rules, and one draw needn't show every extreme that they name: Tile t is held by tile device t // 8. Its west and east neighbours always exist and are tiles of the previous and next tile device, wrapping around; its south and north neighbours are tiles of the same device or -1. The relation is symmetric (west against east, south against north).
All inputs are finite; a program needn't handle non-finite values. No bound on the sum of `land_mask` on one device may be relied on, other than what follows from the above.
Results may differ from the reference program's by a relative error of at most 0.0015.
Values may be sent and summed in bfloat16 or wider, within the bound.
A program may use at most 64 MiB of HBM per device.

```python
import math
import jax
import jax.numpy as jnp
from jax import lax

SLOTS = 8
TILE_ROWS = 128
TILE_COLS = 128
TRACERS = 2
PASSES = 4
MEMBERS = 16
NT = 256


def draw_neighbours(key, part):
    key = jax.random.fold_in(key, 7)
    devices = NT // SLOTS
    first_key, second_key = jax.random.split(key)
    scores = jax.random.randint(first_key, (devices, SLOTS), 0, 1 << 20) * SLOTS + jnp.arange(SLOTS, dtype=jnp.int32)[None, :]
    slot_of = jnp.argsort(scores, axis=1).astype(jnp.int32)
    open_links = jax.random.randint(second_key, (devices, SLOTS), 0, 4) > 0
    dev_index = jnp.arange(devices, dtype=jnp.int32)[:, None]
    row_index = jnp.arange(SLOTS, dtype=jnp.int32)[None, :]
    own_tile = dev_index * SLOTS + slot_of
    west_tile = (dev_index - 1) % devices * SLOTS + jnp.roll(slot_of, 1, axis=0)
    east_tile = (dev_index + 1) % devices * SLOTS + jnp.roll(slot_of, -1, axis=0)
    below = jnp.roll(own_tile, 1, axis=1)
    above = jnp.roll(own_tile, -1, axis=1)
    south_ok = (row_index > 0) & jnp.roll(open_links, 1, axis=1)
    north_ok = (row_index < SLOTS - 1) & open_links
    south_tile = jnp.where(south_ok, below, -1)
    north_tile = jnp.where(north_ok, above, -1)
    rows_table = jnp.stack([west_tile, east_tile, south_tile, north_tile], -1).reshape(NT, 4)
    result = jnp.zeros((NT, 4), jnp.int32).at[own_tile.reshape(NT)].set(rows_table.astype(jnp.int32))
    return result.astype(jnp.int32)


def set_ends(array, stream_key, least, largest):
    index_at = [jax.random.randint(jax.random.fold_in(stream_key, axis), (), 0, length) for axis, length in enumerate(array.shape)]
    main_axis = array.shape.index(max(array.shape))
    next_to = index_at[:main_axis] + [(index_at[main_axis] + 1) % array.shape[main_axis]] + index_at[main_axis + 1:]
    return array.at[tuple(index_at)].set(least).at[tuple(next_to)].set(largest)


def strengthened(values, own_key, source, target, parts, factor):
    owner, partner = [(jnp.arange(values.shape[dim]) // (values.shape[dim] // parts)).reshape([-1 if axis == dim else 1 for axis in range(values.ndim)]) for dim in (source, target)]
    chosen = jax.random.permutation(own_key, parts)[partner]
    strong = (owner == chosen) | (owner == (partner + parts // 2) % parts)
    return jnp.where(strong, factor * values, values)


def block_scale(stream_key, shape, cuts, smallest, largest):
    def one(position, blocks):
        steps = jax.random.uniform(jax.random.fold_in(jax.random.fold_in(stream_key, 6), position), (blocks,), jnp.float32, smallest / len(cuts), largest / len(cuts))
        return jnp.repeat(jnp.exp(steps), shape[position] // blocks).reshape((-1,) + (1,) * (len(shape) - position - 1))

    loudness = one(*cuts[0])
    for cut in cuts[1:]:
        loudness = loudness * one(*cut)
    return loudness


def centred(rng, shape, scale, limit, cuts=(), kind=jnp.bfloat16):
    array = jax.random.normal(rng, shape, jnp.float32) * scale
    if len(cuts) > 0:
        array = block_scale(rng, shape, cuts, -0.22, 0.18) * array
    return jnp.clip(array, min=-limit, max=limit).astype(kind)


def bell_draw_with(rng, dims, scale, reach, pieces, heavy, kind=jnp.bfloat16):
    entries = scale * jax.random.normal(rng, dims, jnp.float32)
    if pieces:
        entries = entries * block_scale(rng, dims, pieces, -0.22, 0.18)
    return jnp.clip(strengthened(entries, jax.random.fold_in(rng, 3), *heavy), -reach, reach).astype(kind)


def setup_inputs(seed: int = 0) -> dict:
    arg_keys = jax.random.split(jax.random.key(seed), 6)
    return {
        "anomalies": centred(arg_keys[0], (MEMBERS, NT, TRACERS, TILE_ROWS, TILE_COLS), 1.0, 6.0, ((0, 16), (1, 32))),
        "weights": bell_draw_with(arg_keys[1], (MEMBERS, NT, MEMBERS), MEMBERS ** -0.5, 2.0, ((0, 16), (1, 32)), (0, 2, 16, 2.0)),
        "diffusivity": jnp.clip(jnp.exp(math.log(1.2) - 3.1780539 * jax.random.uniform(arg_keys[2], (NT, TILE_ROWS, TILE_COLS), jnp.float32) ** block_scale(arg_keys[2], (NT, TILE_ROWS, TILE_COLS), ((0, 32),), -0.2, 0.2)), 0.05, 1.2),
        "land_mask": set_ends((jax.random.randint(arg_keys[3], (NT, TILE_ROWS, TILE_COLS), 0, 5) < 4).astype(jnp.int32), jax.random.fold_in(arg_keys[3], 1), 0, 1),
        "neighbours": draw_neighbours(jax.random.fold_in(arg_keys[5], 71), 0),
    }


diffusion_rate = 0.2

def assemble(tracer_field, west_edge, east_edge, south_edge, north_edge):
    middle = jnp.concatenate([west_edge[..., None], tracer_field, east_edge[..., None]], axis=-1)
    spread = [(0, 0)] * (south_edge.ndim - 1) + [(1, 1)]
    south_edge = jnp.pad(south_edge, spread)
    north_edge = jnp.pad(north_edge, spread)
    return jnp.concatenate([south_edge[..., None, :], middle, north_edge[..., None, :]], axis=-2)

def extend(tracer_field, neighbours):
    present = (neighbours >= 0).astype(tracer_field.dtype)
    safe_index = jnp.maximum(neighbours, 0).astype(jnp.int32)
    west_tiles = jnp.take(tracer_field, safe_index[:, 0], axis=1)
    east_tiles = jnp.take(tracer_field, safe_index[:, 1], axis=1)
    south_tiles = jnp.take(tracer_field, safe_index[:, 2], axis=1)
    north_tiles = jnp.take(tracer_field, safe_index[:, 3], axis=1)
    west_edge = west_tiles[..., :, -1] * present[:, 0][None, :, None, None]
    east_edge = east_tiles[..., :, 0] * present[:, 1][None, :, None, None]
    south_edge = south_tiles[..., -1, :] * present[:, 2][None, :, None, None]
    north_edge = north_tiles[..., 0, :] * present[:, 3][None, :, None, None]
    return assemble(tracer_field, west_edge, east_edge, south_edge, north_edge)

def face_weights(padded):
    centre = padded[..., 1:-1, 1:-1]
    return (jnp.sqrt(centre * padded[..., 1:-1, 2:]), jnp.sqrt(centre * padded[..., 1:-1, :-2]), jnp.sqrt(centre * padded[..., 2:, 1:-1]), jnp.sqrt(centre * padded[..., :-2, 1:-1]))

def reference(anomalies, weights, diffusivity, land_mask, neighbours):
    wet_cells = land_mask.astype(jnp.float32)
    summed = jnp.einsum('ktcij,ktm->mtcij', anomalies.astype(jnp.float32), weights.astype(jnp.float32), precision=lax.Precision.HIGHEST)
    increment = summed * wet_cells[None, :, None]
    coefficient = (diffusivity * wet_cells)[None, :, None]
    east_w, west_w, north_w, south_w = face_weights(extend(coefficient, neighbours))
    for sweep_index in range(PASSES):
        padded = extend(increment, neighbours)
        change = east_w * (padded[..., 1:-1, 2:] - increment) + west_w * (padded[..., 1:-1, :-2] - increment)
        change = change + north_w * (padded[..., 2:, 1:-1] - increment) + south_w * (padded[..., :-2, 1:-1] - increment)
        increment = increment + diffusion_rate * change
    return increment.astype(jnp.bfloat16)
```

```python
import functools

import jax
import jax.numpy as jnp
from jax import lax
from jax.experimental import pallas as pl
from jax.experimental.pallas import tpu as pltpu
from jax.sharding import PartitionSpec as P

MESH = pl.DeviceIdType.MESH
F32 = jnp.float32

RATE = 0.2
SLOTS = 8
N = 128
TRACERS = 2
UNITS = TRACERS * SLOTS
RAW = 3
SUMMED = UNITS - RAW
TRAVEL = UNITS + RAW
RING = 8
LAG = 2
Y_LAG = 6
LAST = 4 * LAG
STEPS = max(TRAVEL + LAST, SUMMED + LAST + Y_LAG)
TOP = 16
PAD = 160
ZERO = SLOTS


def kernel(
    anomalies,
    weights,
    diffusivity,
    land_mask,
    neighbours,
    out,
    blocks,
    own_w,
    splat,
    own_sum,
    away_sum,
    here_sum,
    first,
    second,
    root,
    keep,
    gain,
    inverse,
    diff_in,
    mask_in,
    strips_0,
    strips_1,
    strips_root,
    tables,
    links,
    z_send,
    z_recv,
    w_send,
    w_recv,
    y_send,
    y_recv,
    s_send,
    s_recv,
    t_send,
    t_recv,
    load,
):
    member = lax.axis_index("member")
    tile = lax.axis_index("tile")
    strips = (strips_0, strips_1, strips_root)
    half, z = member // RING, lax.rem(member, RING)
    partner = lax.rem(member + RING, 2 * RING)
    up = (half * RING + lax.rem(z + 1, RING), tile)
    down = (half * RING + lax.rem(z + RING - 1, RING), tile)
    across = (partner, tile)
    tile_devices = lax.axis_size("tile")
    before = lax.rem(tile + tile_devices - 1, tile_devices)
    behind = lax.rem(tile + 1, tile_devices)
    west, east = (member, before), (member, behind)

    def remote(src, dst, send, recv, device):
        return pltpu.make_async_remote_copy(
            src_ref=src,
            dst_ref=dst,
            send_sem=send,
            recv_sem=recv,
            device_id=device,
            device_id_type=MESH,
        )

    loads = [
        pltpu.make_async_copy(
            anomalies.at[:, c], blocks.at[0, pl.ds(c * SLOTS, SLOTS)], load.at[c]
        )
        for c in range(TRACERS)
    ]
    loads.append(pltpu.make_async_copy(diffusivity, diff_in, load.at[TRACERS]))
    loads.append(pltpu.make_async_copy(land_mask, mask_in, load.at[TRACERS + 1]))
    for copy in loads:
        copy.start()

    barrier = pltpu.get_barrier_semaphore()
    for device in (up, down, across, west, east):
        pl.semaphore_signal(barrier, inc=1, device_id=device, device_id_type=MESH)

    spread = (
        lax.broadcasted_iota(jnp.int32, (16, N), 0)
        == lax.broadcasted_iota(jnp.int32, (16, N), 1)
    ).astype(jnp.bfloat16)
    padded = jnp.dot(weights[...], spread, preferred_element_type=F32)
    own_w[0, 0] = jnp.concatenate([padded, jnp.zeros_like(padded)], axis=0).astype(
        jnp.bfloat16
    )
    pl.semaphore_wait(barrier, 5)

    def ring(v, slot):
        rightward = slot < RING // 2
        return remote(
            blocks.at[slot - 1 if rightward else (slot + 1) % RING, v],
            blocks.at[slot, v],
            z_send.at[v * RING + slot],
            z_recv.at[v * RING + slot],
            up if rightward else down,
        )

    def ring_far_right(v):
        return remote(
            blocks.at[3, v], blocks.at[4, v], z_send.at[v * RING + 4], z_recv.at[v * RING + 4], up
        )

    def ring_far_left(v):
        return remote(
            blocks.at[5, v], blocks.at[4, v], z_send.at[v * RING + 4], z_recv.at[v * RING + 4], down
        )

    def ring_w(g, slot):
        rightward = slot <= RING // 2
        return remote(
            own_w.at[g, slot - 1 if rightward else (slot + 1) % RING],
            own_w.at[g, slot],
            w_send.at[g * RING + slot],
            w_recv.at[g * RING + slot],
            up if rightward else down,
        )

    def cross_raw(k):
        return remote(
            anomalies.at[SUMMED + k - SLOTS, 1], blocks.at[0, UNITS + k], y_send.at[UNITS + k], y_recv.at[UNITS + k], across
        )

    def cross_w():
        return remote(own_w.at[0, 0], own_w.at[1, 0], w_send.at[RING], w_recv.at[RING], across)

    def cross_sum(u):
        return remote(away_sum.at[u], here_sum.at[u], y_send.at[u], y_recv.at[u], across)

    def strip_copies(field, c):
        return (
            remote(
                field.at[pl.ds(0, SLOTS), pl.ds(TOP, 8)], strips[c].at[1], s_send.at[c * 2], s_recv.at[c * 2], west
            ),
            remote(
                field.at[pl.ds(0, SLOTS), pl.ds(TOP + N - 8, 8)],
                strips[c].at[0],
                s_send.at[c * 2 + 1],
                s_recv.at[c * 2 + 1],
                east,
            ),
        )

    def table_copies():
        return (
            remote(neighbours, tables.at[1], t_send.at[0], t_recv.at[0], west),
            remote(neighbours, tables.at[0], t_send.at[1], t_recv.at[1], east),
        )

    def send_own(s):
        ring(s, 1).start()
        ring(s, RING - 1).start()

    def send_first(v):
        for slot, device in ((1, up), (RING - 1, down)):
            remote(
                anomalies.at[v, 0], blocks.at[slot, v], z_send.at[v * RING + slot], z_recv.at[v * RING + slot], device
            ).start()

    send_first(0)
    ring_w(0, 1).start()
    ring_w(0, RING - 1).start()
    send_first(1)
    cross_w().start()
    for k in range(RAW):
        cross_raw(k).start()
    for copy in table_copies():
        copy.start()
    for copy in loads:
        copy.wait()

    root[ZERO] = jnp.zeros((PAD, N), F32)
    for field in (first, second):
        for c in range(TRACERS):
            field[c, ZERO] = jnp.zeros((PAD, N), F32)

    @pl.loop(0, SLOTS)
    def _(t):
        coefficient = diff_in[t] * mask_in[t].astype(F32)
        side = jnp.sqrt(RATE * coefficient).T
        root[t, pl.ds(TOP, N)] = side
        wet = side > 0
        inverse[t] = jnp.where(wet, 1.0 / jnp.where(wet, side, 1.0), 0.0)

    for copy in strip_copies(root, TRACERS):
        copy.start()

    lane = lax.broadcasted_iota(jnp.int32, (8, N), 1)

    def set_splat(g, row, owner):
        for s in range(RING):
            w = own_w[g, s].astype(F32)[:SLOTS]
            chosen = jnp.sum(jnp.where(lane == owner, w, 0.0), axis=1, keepdims=True)
            splat[row, s] = jnp.broadcast_to(chosen, (SLOTS, N))

    def sum_unit(u):
        t = lax.rem(u, SLOTS)
        mine = [splat[0, s, pl.ds(t, 1)] for s in range(RING)]
        theirs = [splat[1, s, pl.ds(t, 1)] for s in range(RING)]

        @pl.loop(0, N // 16)
        def _(i):
            rows = pl.ds(pl.multiple_of(i * 16, 16), 16)
            for s in range(RING):
                x = blocks[s, u, rows].astype(F32)
                if s == 0:
                    a, b = x * mine[s], x * theirs[s]
                else:
                    a, b = a + x * mine[s], b + x * theirs[s]
            own_sum[u, rows] = a
            away_sum[u, rows] = b

    def sum_raw(k):
        u = SUMMED + k
        t = lax.rem(u, SLOTS)
        mine = [splat[0, s, pl.ds(t, 1)] for s in range(RING)]
        theirs = [splat[2, s, pl.ds(t, 1)] for s in range(RING)]

        @pl.loop(0, N // 16)
        def _(i):
            rows = pl.ds(pl.multiple_of(i * 16, 16), 16)
            for s in range(RING):
                x, y = blocks[s, u, rows].astype(F32), blocks[s, UNITS + k, rows].astype(F32)
                if s == 0:
                    a = x * mine[s] + y * theirs[s]
                else:
                    a = a + (x * mine[s] + y * theirs[s])
            own_sum[u, rows] = a

    def place(u, total):
        c, t = u // SLOTS, lax.rem(u, SLOTS)
        first[c, t, pl.ds(TOP, N)] = total.T * root[t, pl.ds(TOP, N)]

    def unpack(field, c):
        @pl.loop(0, SLOTS)
        def _(t):
            field[t, pl.ds(TOP - 8, 8)] = strips[c][0, links[t, 0]]
            field[t, pl.ds(TOP + N, 8)] = strips[c][1, links[t, 1]]

    def read_tables():
        for copy in table_copies():
            copy.wait()
        def local(index):
            return jnp.where(index < 0, ZERO, lax.rem(jnp.maximum(index, 0), SLOTS))

        @pl.loop(0, SLOTS)
        def _(t):
            w, e = (lax.rem(jnp.maximum(neighbours[t, k], 0), SLOTS) for k in (0, 1))
            links[t, 0] = w
            links[t, 1] = e
            for k in (2, 3):
                links[t, k] = local(neighbours[t, k])
                for side, slot, back, at in ((0, w, 1, 2), (1, e, 0, 4)):
                    beyond = tables[side, slot, k]
                    via = tables[side, lax.rem(jnp.maximum(beyond, 0), SLOTS), back]
                    links[t, at + k] = jnp.where(beyond < 0, ZERO, local(via))

    lane16 = lax.broadcasted_iota(jnp.int32, (16, N), 1)

    def around(field, t, r, size, south, north):
        lanes = lane16[:size]
        y = field[t, pl.ds(r, size)]
        to_north = pltpu.roll(jnp.where(lanes == 0, field[north, pl.ds(r, size)], y), N - 1, 1)
        to_south = pltpu.roll(jnp.where(lanes == N - 1, field[south, pl.ds(r, size)], y), 1, 1)
        return (field[t, pl.ds(r + 1, size)] + field[t, pl.ds(r - 1, size)]) + (to_north + to_south)

    def pieces(t, with_strips):
        if with_strips:
            yield TOP - 8, 8, links[t, 4], links[t, 5]
        for r in range(TOP, TOP + N, 16):
            yield r, 16, links[t, 2], links[t, 3]
        if with_strips:
            yield TOP + N, 8, links[t, 6], links[t, 7]

    def set_gains():
        for copy in strip_copies(root, TRACERS):
            copy.wait()
        read_tables()
        unpack(root, TRACERS)

        @pl.loop(0, SLOTS)
        def _(t):
            for r, size, south, north in pieces(t, True):
                side = root[t, pl.ds(r, size)]
                keep[t, pl.ds(r, size)] = 1.0 - side * around(root, t, r, size, south, north)
                gain[t, pl.ds(r, size)] = side * side

    def sweep(source, target, c, with_strips):
        here, there = source.at[c], target.at[c]

        @pl.loop(0, SLOTS)
        def _(t):
            for r, size, south, north in pieces(t, with_strips):
                rows = pl.ds(r, size)
                there[t, rows] = keep[t, rows] * here[t, rows] + gain[t, rows] * around(
                    here, t, r, size, south, north
                )

    def begin(c):
        for copy in strip_copies(first.at[c], c):
            copy.start()

    def arrived(c):
        for copy in strip_copies(first.at[c], c):
            copy.wait()
        unpack(first.at[c], c)

    def finish(c):
        here = first.at[c]

        @pl.loop(0, SLOTS)
        def _(t):
            rows = pl.ds(TOP, N)
            out[t, c] = (here[t, rows] * inverse[t]).T.astype(jnp.bfloat16)

    def step(s):
        for d in (3, 2, 1):
            v = s - LAG * d

            @pl.when(jnp.logical_and(v >= 0, v < TRAVEL))
            def _():
                ring(v, d).wait_recv()
                if d < 3:
                    ring(v, d + 1).start()
                else:

                    @pl.when(lax.rem(v, 2) == 0)
                    def _():
                        ring_far_right(v).start()

                ring(v, RING - d).wait_recv()
                if d < 3:
                    ring(v, RING - d - 1).start()
                else:

                    @pl.when(lax.rem(v, 2) == 1)
                    def _():
                        ring_far_left(v).start()

            for g, at in ((0, 0), (1, UNITS)):

                @pl.when(v == at)
                def _():
                    ring_w(g, d).wait_recv()
                    ring_w(g, d + 1).start()
                    ring_w(g, RING - d).wait_recv()
                    if d < 3:
                        ring_w(g, RING - d - 1).start()

        @pl.when(s == UNITS)
        def _():
            cross_w().wait_recv()
            ring_w(1, 1).start()
            ring_w(1, RING - 1).start()

        @pl.when(jnp.logical_and(s >= UNITS, s < TRAVEL))
        def _():
            cross_raw(s - UNITS).wait_recv()

        @pl.when(s < TRAVEL)
        def _():
            send_own(s)

        v = s - LAST

        @pl.when(v == 0)
        def _():
            ring_w(0, 4).wait_recv()
            set_splat(0, 0, member)
            set_splat(0, 1, partner)

        @pl.when(v == UNITS)
        def _():
            ring_w(1, 4).wait_recv()
            set_splat(1, 2, member)

        @pl.when(jnp.logical_and(v >= 0, v < TRAVEL))
        def _():
            ring_far_right(v).wait_recv()

        @pl.when(jnp.logical_and(v >= 0, v < SUMMED))
        def _():
            sum_unit(v)
            cross_sum(v).start()

        @pl.when(jnp.logical_and(v >= UNITS, v < TRAVEL))
        def _():
            k = v - UNITS
            sum_raw(k)
            place(SUMMED + k, own_sum[SUMMED + k])

        u = v - Y_LAG

        @pl.when(jnp.logical_and(u >= 0, u < SUMMED))
        def _():
            cross_sum(u).wait_recv()
            place(u, own_sum[u] + here_sum[u])

        @pl.when(s == LAST + 2)
        def _():
            set_gains()

        @pl.when(u == SLOTS - 1)
        def _():
            begin(0)

    pl.loop(2, STEPS)(step)

    begin(1)

    arrived(0)
    sweep(first, second, 0, True)
    sweep(second, first, 0, True)
    sweep(first, second, 0, True)
    sweep(second, first, 0, False)
    finish(0)

    @pl.loop(0, TRAVEL)
    def _(v):
        for slot in (1, 2, 3, 5, 6, 7):
            ring(v, slot).wait_send()
        ring_far_right(v).wait_send()

    for g in range(2):
        for slot in range(1, RING):
            ring_w(g, slot).wait_send()
    cross_w().wait_send()

    @pl.loop(0, SUMMED)
    def _(u):
        cross_sum(u).wait_send()

    for k in range(RAW):
        cross_raw(k).wait_send()

    arrived(1)
    sweep(first, second, 1, True)
    sweep(second, first, 1, True)
    sweep(first, second, 1, True)
    sweep(second, first, 1, False)
    finish(1)


def shards(anomalies, weights, diffusivity, land_mask, neighbours):
    anywhere = pl.BlockSpec(memory_space=pl.ANY)
    vmem = pl.BlockSpec(memory_space=pltpu.VMEM)
    smem = pl.BlockSpec(memory_space=pltpu.SMEM)
    result = pl.pallas_call(
        kernel,
        out_shape=jax.ShapeDtypeStruct((SLOTS, TRACERS, N, N), jnp.bfloat16),
        in_specs=[anywhere, vmem, anywhere, anywhere, smem],
        out_specs=vmem,
        scratch_shapes=[
            pltpu.VMEM((RING, TRAVEL, N, N), jnp.bfloat16),
            pltpu.VMEM((2, RING, 16, N), jnp.bfloat16),
            pltpu.VMEM((3, RING, SLOTS, N), F32),
            pltpu.VMEM((UNITS, N, N), F32),
            pltpu.VMEM((SUMMED, N, N), F32),
            pltpu.VMEM((SUMMED, N, N), F32),
            pltpu.VMEM((TRACERS, SLOTS + 1, PAD, N), F32),
            pltpu.VMEM((TRACERS, SLOTS + 1, PAD, N), F32),
            pltpu.VMEM((SLOTS + 1, PAD, N), F32),
            pltpu.VMEM((SLOTS, PAD, N), F32),
            pltpu.VMEM((SLOTS, PAD, N), F32),
            pltpu.VMEM((SLOTS, N, N), F32),
            pltpu.VMEM((SLOTS, N, N), F32),
            pltpu.VMEM((SLOTS, N, N), jnp.int32),
            pltpu.VMEM((2, SLOTS, 8, N), F32),
            pltpu.VMEM((2, SLOTS, 8, N), F32),
            pltpu.VMEM((2, SLOTS, 8, N), F32),
            pltpu.SMEM((2, SLOTS, 4), jnp.int32),
            pltpu.SMEM((SLOTS, 8), jnp.int32),
            pltpu.SemaphoreType.DMA((TRAVEL * RING,)),
            pltpu.SemaphoreType.DMA((TRAVEL * RING,)),
            pltpu.SemaphoreType.DMA((2 * RING,)),
            pltpu.SemaphoreType.DMA((2 * RING,)),
            pltpu.SemaphoreType.DMA((TRAVEL,)),
            pltpu.SemaphoreType.DMA((TRAVEL,)),
            pltpu.SemaphoreType.DMA((2 * TRACERS + 2,)),
            pltpu.SemaphoreType.DMA((2 * TRACERS + 2,)),
            pltpu.SemaphoreType.DMA((2,)),
            pltpu.SemaphoreType.DMA((2,)),
            pltpu.SemaphoreType.DMA((TRACERS + 2,)),
        ],
        compiler_params=pltpu.CompilerParams(
            collective_id=0, has_side_effects=True, vmem_limit_bytes=48 << 20
        ),
    )(anomalies[0], weights[0], diffusivity, land_mask, neighbours)
    return result[None]


def solution(mesh):
    return jax.shard_map(
        shards,
        mesh=mesh,
        in_specs=(
            P("member", "tile", None, None, None),
            P("member", "tile", None),
            P("tile", None, None),
            P("tile", None, None),
            P("tile", None),
        ),
        out_specs=P("member", "tile", None, None, None),
        check_vma=False,
    )
```

```python
import functools

import jax
import jax.numpy as jnp
from jax import lax
from jax.experimental import pallas as pl
from jax.experimental.pallas import tpu as pltpu
from jax.sharding import PartitionSpec as P

MESH = pl.DeviceIdType.MESH
F32 = jnp.float32

RATE = 0.2
SLOTS = 8
N = 128
TRACERS = 2
UNITS = TRACERS * SLOTS
RAW = 3
SUMMED = UNITS - RAW
TRAVEL = UNITS + RAW
RING = 8
LAG = 2
Y_LAG = 6
LAST = 4 * LAG
STEPS = max(TRAVEL + LAST, SUMMED + LAST + Y_LAG)
TOP = 16
PAD = 160
ZERO = SLOTS


def kernel(
    anomalies,
    weights,
    diffusivity,
    land_mask,
    neighbour_table,
    out,
    blocks,
    own_w,
    splat,
    own_sum,
    away_sum,
    here_sum,
    first,
    second,
    root,
    keep,
    gain,
    inverse,
    diff_in,
    mask_in,
    strips_0,
    strips_1,
    strips_root,
    tables,
    links,
    neighbours,
    weights_in,
    z_send,
    z_recv,
    w_send,
    w_recv,
    y_send,
    y_recv,
    s_send,
    s_recv,
    t_send,
    t_recv,
    load,
):
    member = lax.axis_index("member")
    tile = lax.axis_index("tile")
    strips = (strips_0, strips_1, strips_root)
    half, z = member // RING, lax.rem(member, RING)
    partner = lax.rem(member + RING, 2 * RING)
    up = (half * RING + lax.rem(z + 1, RING), tile)
    down = (half * RING + lax.rem(z + RING - 1, RING), tile)
    across = (partner, tile)
    tile_devices = lax.axis_size("tile")
    before = lax.rem(tile + tile_devices - 1, tile_devices)
    behind = lax.rem(tile + 1, tile_devices)
    west, east = (member, before), (member, behind)

    def remote(src, dst, send, recv, device):
        return pltpu.make_async_remote_copy(
            src_ref=src,
            dst_ref=dst,
            send_sem=send,
            recv_sem=recv,
            device_id=device,
            device_id_type=MESH,
        )

    barrier = pltpu.get_barrier_semaphore()
    for device in (up, down, across, west, east):
        pl.semaphore_signal(barrier, inc=1, device_id=device, device_id_type=MESH)

    loads = [
        pltpu.make_async_copy(weights, weights_in, load.at[0]),
        pltpu.make_async_copy(neighbour_table, neighbours, load.at[1]),
        pltpu.make_async_copy(diffusivity, diff_in, load.at[2]),
        pltpu.make_async_copy(land_mask, mask_in, load.at[3]),
    ]
    for c in range(TRACERS):
        loads.append(
            pltpu.make_async_copy(
                anomalies.at[:, c], blocks.at[0, pl.ds(c * SLOTS, SLOTS)], load.at[4 + c]
            )
        )
    for copy in loads:
        copy.start()
    pl.semaphore_wait(barrier, 5)

    def ring(v, slot):
        rightward = slot < RING // 2
        return remote(
            blocks.at[slot - 1 if rightward else (slot + 1) % RING, v],
            blocks.at[slot, v],
            z_send.at[v * RING + slot],
            z_recv.at[v * RING + slot],
            up if rightward else down,
        )

    def ring_far_right(v):
        return remote(
            blocks.at[3, v], blocks.at[4, v], z_send.at[v * RING + 4], z_recv.at[v * RING + 4], up
        )

    def ring_far_left(v):
        return remote(
            blocks.at[5, v], blocks.at[4, v], z_send.at[v * RING + 4], z_recv.at[v * RING + 4], down
        )

    def ring_w(g, slot):
        rightward = slot <= RING // 2
        return remote(
            own_w.at[g, slot - 1 if rightward else (slot + 1) % RING],
            own_w.at[g, slot],
            w_send.at[g * RING + slot],
            w_recv.at[g * RING + slot],
            up if rightward else down,
        )

    def cross_raw(k):
        return remote(
            anomalies.at[SUMMED + k - SLOTS, 1], blocks.at[0, UNITS + k], y_send.at[UNITS + k], y_recv.at[UNITS + k], across
        )

    def cross_w():
        return remote(own_w.at[0, 0], own_w.at[1, 0], w_send.at[RING], w_recv.at[RING], across)

    def cross_sum(u):
        return remote(away_sum.at[u], here_sum.at[u], y_send.at[u], y_recv.at[u], across)

    def strip_copies(field, c):
        return (
            remote(
                field.at[pl.ds(0, SLOTS), pl.ds(TOP, 8)], strips[c].at[1], s_send.at[c * 2], s_recv.at[c * 2], west
            ),
            remote(
                field.at[pl.ds(0, SLOTS), pl.ds(TOP + N - 8, 8)],
                strips[c].at[0],
                s_send.at[c * 2 + 1],
                s_recv.at[c * 2 + 1],
                east,
            ),
        )

    def table_copies():
        return (
            remote(neighbours, tables.at[1], t_send.at[0], t_recv.at[0], west),
            remote(neighbours, tables.at[0], t_send.at[1], t_recv.at[1], east),
        )

    def send_own(s):
        ring(s, 1).start()
        ring(s, RING - 1).start()

    def send_first(v):
        for slot, device in ((1, up), (RING - 1, down)):
            remote(
                anomalies.at[v, 0], blocks.at[slot, v], z_send.at[v * RING + slot], z_recv.at[v * RING + slot], device
            ).start()

    send_first(0)
    send_first(1)
    for k in range(RAW):
        cross_raw(k).start()

    loads[0].wait()
    spread = (
        lax.broadcasted_iota(jnp.int32, (16, N), 0)
        == lax.broadcasted_iota(jnp.int32, (16, N), 1)
    ).astype(jnp.bfloat16)
    padded = jnp.dot(weights_in[...], spread, preferred_element_type=F32)
    own_w[0, 0] = jnp.concatenate([padded, jnp.zeros_like(padded)], axis=0).astype(
        jnp.bfloat16
    )
    ring_w(0, 1).start()
    ring_w(0, RING - 1).start()
    cross_w().start()
    loads[1].wait()
    for copy in table_copies():
        copy.start()
    for copy in loads[2:]:
        copy.wait()

    root[ZERO] = jnp.zeros((PAD, N), F32)
    for field in (first, second):
        for c in range(TRACERS):
            field[c, ZERO] = jnp.zeros((PAD, N), F32)

    @pl.loop(0, SLOTS)
    def _(t):
        coefficient = diff_in[t] * mask_in[t].astype(F32)
        side = jnp.sqrt(RATE * coefficient).T
        root[t, pl.ds(TOP, N)] = side
        wet = side > 0
        inverse[t] = jnp.where(wet, 1.0 / jnp.where(wet, side, 1.0), 0.0)

    for copy in strip_copies(root, TRACERS):
        copy.start()

    lane = lax.broadcasted_iota(jnp.int32, (8, N), 1)

    def set_splat(g, row, owner):
        for s in range(RING):
            w = own_w[g, s].astype(F32)[:SLOTS]
            chosen = jnp.sum(jnp.where(lane == owner, w, 0.0), axis=1, keepdims=True)
            splat[row, s] = jnp.broadcast_to(chosen, (SLOTS, N))

    def sum_unit(u):
        t = lax.rem(u, SLOTS)
        mine = [splat[0, s, pl.ds(t, 1)] for s in range(RING)]
        theirs = [splat[1, s, pl.ds(t, 1)] for s in range(RING)]

        @pl.loop(0, N // 16)
        def _(i):
            rows = pl.ds(pl.multiple_of(i * 16, 16), 16)
            for s in range(RING):
                x = blocks[s, u, rows].astype(F32)
                if s == 0:
                    a, b = x * mine[s], x * theirs[s]
                else:
                    a, b = a + x * mine[s], b + x * theirs[s]
            own_sum[u, rows] = a
            away_sum[u, rows] = b

    def sum_raw(k):
        u = SUMMED + k
        t = lax.rem(u, SLOTS)
        mine = [splat[0, s, pl.ds(t, 1)] for s in range(RING)]
        theirs = [splat[2, s, pl.ds(t, 1)] for s in range(RING)]

        @pl.loop(0, N // 16)
        def _(i):
            rows = pl.ds(pl.multiple_of(i * 16, 16), 16)
            for s in range(RING):
                x, y = blocks[s, u, rows].astype(F32), blocks[s, UNITS + k, rows].astype(F32)
                if s == 0:
                    a = x * mine[s] + y * theirs[s]
                else:
                    a = a + (x * mine[s] + y * theirs[s])
            own_sum[u, rows] = a

    def place(u, total):
        c, t = u // SLOTS, lax.rem(u, SLOTS)
        first[c, t, pl.ds(TOP, N)] = total.T * root[t, pl.ds(TOP, N)]

    def unpack(field, c):
        @pl.loop(0, SLOTS)
        def _(t):
            field[t, pl.ds(TOP - 8, 8)] = strips[c][0, links[t, 0]]
            field[t, pl.ds(TOP + N, 8)] = strips[c][1, links[t, 1]]

    def read_tables():
        for copy in table_copies():
            copy.wait()
        def local(index):
            return jnp.where(index < 0, ZERO, lax.rem(jnp.maximum(index, 0), SLOTS))

        @pl.loop(0, SLOTS)
        def _(t):
            w, e = (lax.rem(jnp.maximum(neighbours[t, k], 0), SLOTS) for k in (0, 1))
            links[t, 0] = w
            links[t, 1] = e
            for k in (2, 3):
                links[t, k] = local(neighbours[t, k])
                for side, slot, back, at in ((0, w, 1, 2), (1, e, 0, 4)):
                    beyond = tables[side, slot, k]
                    via = tables[side, lax.rem(jnp.maximum(beyond, 0), SLOTS), back]
                    links[t, at + k] = jnp.where(beyond < 0, ZERO, local(via))

    lane16 = lax.broadcasted_iota(jnp.int32, (16, N), 1)

    def around(field, t, r, size, south, north):
        lanes = lane16[:size]
        y = field[t, pl.ds(r, size)]
        to_north = pltpu.roll(jnp.where(lanes == 0, field[north, pl.ds(r, size)], y), N - 1, 1)
        to_south = pltpu.roll(jnp.where(lanes == N - 1, field[south, pl.ds(r, size)], y), 1, 1)
        return (field[t, pl.ds(r + 1, size)] + field[t, pl.ds(r - 1, size)]) + (to_north + to_south)

    def pieces(t, with_strips):
        if with_strips:
            yield TOP - 8, 8, links[t, 4], links[t, 5]
        for r in range(TOP, TOP + N, 16):
            yield r, 16, links[t, 2], links[t, 3]
        if with_strips:
            yield TOP + N, 8, links[t, 6], links[t, 7]

    def prepare_gains():
        for copy in strip_copies(root, TRACERS):
            copy.wait()
        read_tables()
        unpack(root, TRACERS)

    def set_gains(t):
        results = []
        for r, size, south, north in pieces(t, True):
            side = root[t, pl.ds(r, size)]
            results.append((r, size, 1.0 - side * around(root, t, r, size, south, north), side * side))
        for r, size, kept, gained in results:
            keep[t, pl.ds(r, size)] = kept
            gain[t, pl.ds(r, size)] = gained

    def sweep(source, target, c, with_strips):
        here, there = source.at[c], target.at[c]

        @pl.loop(0, SLOTS, unroll=2)
        def _(t):
            results = []
            for r, size, south, north in pieces(t, with_strips):
                rows = pl.ds(r, size)
                value = keep[t, rows] * here[t, rows] + gain[t, rows] * around(
                    here, t, r, size, south, north
                )
                results.append((rows, value))
            for rows, value in results:
                there[t, rows] = value

    def begin(c):
        for copy in strip_copies(first.at[c], c):
            copy.start()

    def arrived(c):
        for copy in strip_copies(first.at[c], c):
            copy.wait()
        unpack(first.at[c], c)

    def finish(c):
        here = first.at[c]

        @pl.loop(0, SLOTS, unroll=4)
        def _(t):
            rows = pl.ds(TOP, N)
            out[t, c] = (here[t, rows] * inverse[t]).T.astype(jnp.bfloat16)

    def step(s):
        for d in (3, 2, 1):
            v = s - LAG * d

            @pl.when(jnp.logical_and(v >= 0, v < TRAVEL))
            def _():
                ring(v, d).wait_recv()
                if d < 3:
                    ring(v, d + 1).start()
                else:

                    @pl.when(lax.rem(v, 2) == 0)
                    def _():
                        ring_far_right(v).start()

                ring(v, RING - d).wait_recv()
                if d < 3:
                    ring(v, RING - d - 1).start()
                else:

                    @pl.when(lax.rem(v, 2) == 1)
                    def _():
                        ring_far_left(v).start()

            for g, at in ((0, 0), (1, UNITS)):

                @pl.when(v == at)
                def _():
                    ring_w(g, d).wait_recv()
                    ring_w(g, d + 1).start()
                    ring_w(g, RING - d).wait_recv()
                    if d < 3:
                        ring_w(g, RING - d - 1).start()

        @pl.when(s == UNITS)
        def _():
            cross_w().wait_recv()
            ring_w(1, 1).start()
            ring_w(1, RING - 1).start()

        @pl.when(jnp.logical_and(s >= UNITS, s < TRAVEL))
        def _():
            cross_raw(s - UNITS).wait_recv()

        @pl.when(s < TRAVEL)
        def _():
            send_own(s)

        v = s - LAST

        @pl.when(v == 0)
        def _():
            ring_w(0, 4).wait_recv()
            set_splat(0, 0, member)
            set_splat(0, 1, partner)

        @pl.when(v == UNITS)
        def _():
            ring_w(1, 4).wait_recv()
            set_splat(1, 2, member)

        @pl.when(jnp.logical_and(v >= 0, v < TRAVEL))
        def _():
            ring_far_right(v).wait_recv()

        @pl.when(jnp.logical_and(v >= 0, v < SUMMED))
        def _():
            sum_unit(v)
            cross_sum(v).start()

        @pl.when(jnp.logical_and(v >= UNITS, v < TRAVEL))
        def _():
            k = v - UNITS
            sum_raw(k)
            place(SUMMED + k, own_sum[SUMMED + k])

        u = v - Y_LAG

        @pl.when(jnp.logical_and(u >= 0, u < SUMMED))
        def _():
            cross_sum(u).wait_recv()
            place(u, own_sum[u] + here_sum[u])

        @pl.when(s == LAST + 1)
        def _():
            prepare_gains()

        @pl.when(jnp.logical_and(s >= LAST + 2, s < LAST + 2 + SLOTS))
        def _():
            set_gains(s - (LAST + 2))

        @pl.when(u == SLOTS - 1)
        def _():
            begin(0)

    pl.loop(2, STEPS)(step)

    begin(1)

    arrived(0)
    sweep(first, second, 0, True)
    sweep(second, first, 0, True)
    sweep(first, second, 0, True)
    sweep(second, first, 0, False)
    finish(0)

    @pl.loop(0, TRAVEL)
    def _(v):
        for slot in (1, 2, 3, 5, 6, 7):
            ring(v, slot).wait_send()
        ring_far_right(v).wait_send()

    for g in range(2):
        for slot in range(1, RING):
            ring_w(g, slot).wait_send()
    cross_w().wait_send()

    @pl.loop(0, SUMMED)
    def _(u):
        cross_sum(u).wait_send()

    for k in range(RAW):
        cross_raw(k).wait_send()

    arrived(1)
    sweep(first, second, 1, True)
    sweep(second, first, 1, True)
    sweep(first, second, 1, True)
    sweep(second, first, 1, False)
    finish(1)


def shards(anomalies, weights, diffusivity, land_mask, neighbours):
    anywhere = pl.BlockSpec(memory_space=pl.ANY)
    vmem = pl.BlockSpec(memory_space=pltpu.VMEM)
    result = pl.pallas_call(
        kernel,
        out_shape=jax.ShapeDtypeStruct((SLOTS, TRACERS, N, N), jnp.bfloat16),
        in_specs=[anywhere] * 5,
        out_specs=vmem,
        scratch_shapes=[
            pltpu.VMEM((RING, TRAVEL, N, N), jnp.bfloat16),
            pltpu.VMEM((2, RING, 16, N), jnp.bfloat16),
            pltpu.VMEM((3, RING, SLOTS, N), F32),
            pltpu.VMEM((UNITS, N, N), F32),
            pltpu.VMEM((SUMMED, N, N), F32),
            pltpu.VMEM((SUMMED, N, N), F32),
            pltpu.VMEM((TRACERS, SLOTS + 1, PAD, N), F32),
            pltpu.VMEM((TRACERS, SLOTS + 1, PAD, N), F32),
            pltpu.VMEM((SLOTS + 1, PAD, N), F32),
            pltpu.VMEM((SLOTS, PAD, N), F32),
            pltpu.VMEM((SLOTS, PAD, N), F32),
            pltpu.VMEM((SLOTS, N, N), F32),
            pltpu.VMEM((SLOTS, N, N), F32),
            pltpu.VMEM((SLOTS, N, N), jnp.int32),
            pltpu.VMEM((2, SLOTS, 8, N), F32),
            pltpu.VMEM((2, SLOTS, 8, N), F32),
            pltpu.VMEM((2, SLOTS, 8, N), F32),
            pltpu.SMEM((2, SLOTS, 4), jnp.int32),
            pltpu.SMEM((SLOTS, 8), jnp.int32),
            pltpu.SMEM((SLOTS, 4), jnp.int32),
            pltpu.VMEM((SLOTS, 16), jnp.bfloat16),
            pltpu.SemaphoreType.DMA((TRAVEL * RING,)),
            pltpu.SemaphoreType.DMA((TRAVEL * RING,)),
            pltpu.SemaphoreType.DMA((2 * RING,)),
            pltpu.SemaphoreType.DMA((2 * RING,)),
            pltpu.SemaphoreType.DMA((TRAVEL,)),
            pltpu.SemaphoreType.DMA((TRAVEL,)),
            pltpu.SemaphoreType.DMA((2 * TRACERS + 2,)),
            pltpu.SemaphoreType.DMA((2 * TRACERS + 2,)),
            pltpu.SemaphoreType.DMA((2,)),
            pltpu.SemaphoreType.DMA((2,)),
            pltpu.SemaphoreType.DMA((TRACERS + 4,)),
        ],
        compiler_params=pltpu.CompilerParams(
            collective_id=0, has_side_effects=True, vmem_limit_bytes=48 << 20
        ),
    )(anomalies[0], weights[0], diffusivity, land_mask, neighbours)
    return result[None]


def solution(mesh):
    return jax.shard_map(
        shards,
        mesh=mesh,
        in_specs=(
            P("member", "tile", None, None, None),
            P("member", "tile", None),
            P("tile", None, None),
            P("tile", None, None),
            P("tile", None),
        ),
        out_specs=P("member", "tile", None, None, None),
        check_vma=False,
    )
```

```python
import functools

import jax
import jax.numpy as jnp
from jax import lax
from jax.experimental import pallas as pl
from jax.experimental.pallas import tpu as pltpu
from jax.sharding import PartitionSpec as P

MESH = pl.DeviceIdType.MESH
F32 = jnp.float32

RATE = 0.2
SLOTS = 8
N = 128
TRACERS = 2
UNITS = TRACERS * SLOTS
RAW = 3
SUMMED = UNITS - RAW
TRAVEL = UNITS + RAW
RING = 8
LAGS = (4, 7, 9, 10)
Y_LAG = 6
LAST = LAGS[3]
STEPS = max(TRAVEL + LAST, SUMMED + LAST + Y_LAG)
TOP = 16
PAD = 160
ZERO = SLOTS


def kernel(
    anomalies,
    weights,
    diffusivity,
    land_mask,
    neighbour_table,
    out,
    blocks,
    own_w,
    splat,
    own_sum,
    away_sum,
    here_sum,
    first,
    second,
    root,
    keep,
    gain,
    inverse,
    diff_in,
    mask_in,
    strips_0,
    strips_1,
    strips_root,
    tables,
    links,
    neighbours,
    weights_in,
    z_send,
    z_recv,
    w_send,
    w_recv,
    y_send,
    y_recv,
    s_send,
    s_recv,
    t_send,
    t_recv,
    load,
):
    member = lax.axis_index("member")
    tile = lax.axis_index("tile")
    strips = (strips_0, strips_1, strips_root)
    half, z = member // RING, lax.rem(member, RING)
    partner = lax.rem(member + RING, 2 * RING)
    up = (half * RING + lax.rem(z + 1, RING), tile)
    down = (half * RING + lax.rem(z + RING - 1, RING), tile)
    across = (partner, tile)
    tile_devices = lax.axis_size("tile")
    before = lax.rem(tile + tile_devices - 1, tile_devices)
    behind = lax.rem(tile + 1, tile_devices)
    west, east = (member, before), (member, behind)

    def remote(src, dst, send, recv, device):
        return pltpu.make_async_remote_copy(
            src_ref=src,
            dst_ref=dst,
            send_sem=send,
            recv_sem=recv,
            device_id=device,
            device_id_type=MESH,
        )

    barrier = pltpu.get_barrier_semaphore()
    for device in (up, down, across, west, east):
        pl.semaphore_signal(barrier, inc=1, device_id=device, device_id_type=MESH)

    loads = [
        pltpu.make_async_copy(weights, weights_in, load.at[0]),
        pltpu.make_async_copy(neighbour_table, neighbours, load.at[1]),
        pltpu.make_async_copy(diffusivity, diff_in, load.at[2]),
        pltpu.make_async_copy(land_mask, mask_in, load.at[3]),
    ]
    for c in range(TRACERS):
        loads.append(
            pltpu.make_async_copy(
                anomalies.at[:, c], blocks.at[0, pl.ds(c * SLOTS, SLOTS)], load.at[4 + c]
            )
        )
    for copy in loads:
        copy.start()
    pl.semaphore_wait(barrier, 5)

    def ring(v, slot):
        rightward = slot < RING // 2
        return remote(
            blocks.at[slot - 1 if rightward else (slot + 1) % RING, v],
            blocks.at[slot, v],
            z_send.at[v * RING + slot],
            z_recv.at[v * RING + slot],
            up if rightward else down,
        )

    def ring_far_right(v):
        return remote(
            blocks.at[3, v], blocks.at[4, v], z_send.at[v * RING + 4], z_recv.at[v * RING + 4], up
        )

    def ring_far_left(v):
        return remote(
            blocks.at[5, v], blocks.at[4, v], z_send.at[v * RING + 4], z_recv.at[v * RING + 4], down
        )

    def ring_w(g, slot):
        rightward = slot <= RING // 2
        return remote(
            own_w.at[g, slot - 1 if rightward else (slot + 1) % RING],
            own_w.at[g, slot],
            w_send.at[g * RING + slot],
            w_recv.at[g * RING + slot],
            up if rightward else down,
        )

    def cross_raw(k):
        return remote(
            anomalies.at[SUMMED + k - SLOTS, 1], blocks.at[0, UNITS + k], y_send.at[UNITS + k], y_recv.at[UNITS + k], across
        )

    def cross_w():
        return remote(own_w.at[0, 0], own_w.at[1, 0], w_send.at[RING], w_recv.at[RING], across)

    def cross_sum(u):
        return remote(away_sum.at[u], here_sum.at[u], y_send.at[u], y_recv.at[u], across)

    def strip_copies(field, c):
        return (
            remote(
                field.at[pl.ds(0, SLOTS), pl.ds(TOP, 8)], strips[c].at[1], s_send.at[c * 2], s_recv.at[c * 2], west
            ),
            remote(
                field.at[pl.ds(0, SLOTS), pl.ds(TOP + N - 8, 8)],
                strips[c].at[0],
                s_send.at[c * 2 + 1],
                s_recv.at[c * 2 + 1],
                east,
            ),
        )

    def table_copies():
        return (
            remote(neighbours, tables.at[1], t_send.at[0], t_recv.at[0], west),
            remote(neighbours, tables.at[0], t_send.at[1], t_recv.at[1], east),
        )

    def send_own(s):
        ring(s, 1).start()
        ring(s, RING - 1).start()

    def send_first(v):
        for slot, device in ((1, up), (RING - 1, down)):
            remote(
                anomalies.at[v, 0], blocks.at[slot, v], z_send.at[v * RING + slot], z_recv.at[v * RING + slot], device
            ).start()

    send_first(0)
    send_first(1)
    for k in range(RAW):
        cross_raw(k).start()

    loads[0].wait()
    spread = (
        lax.broadcasted_iota(jnp.int32, (16, N), 0)
        == lax.broadcasted_iota(jnp.int32, (16, N), 1)
    ).astype(jnp.bfloat16)
    padded = jnp.dot(weights_in[...], spread, preferred_element_type=F32)
    own_w[0, 0] = jnp.concatenate([padded, jnp.zeros_like(padded)], axis=0).astype(
        jnp.bfloat16
    )
    ring_w(0, 1).start()
    ring_w(0, RING - 1).start()
    cross_w().start()
    loads[1].wait()
    for copy in table_copies():
        copy.start()
    for copy in loads[2:]:
        copy.wait()

    root[ZERO] = jnp.zeros((PAD, N), F32)
    for field in (first, second):
        for c in range(TRACERS):
            field[c, ZERO] = jnp.zeros((PAD, N), F32)

    @pl.loop(0, SLOTS)
    def _(t):
        coefficient = diff_in[t] * mask_in[t].astype(F32)
        side = jnp.sqrt(RATE * coefficient).T
        root[t, pl.ds(TOP, N)] = side
        wet = side > 0
        inverse[t] = jnp.where(wet, 1.0 / jnp.where(wet, side, 1.0), 0.0)

    for copy in strip_copies(root, TRACERS):
        copy.start()

    lane = lax.broadcasted_iota(jnp.int32, (8, N), 1)

    def set_splat(g, row, owner):
        for s in range(RING):
            w = own_w[g, s].astype(F32)[:SLOTS]
            chosen = jnp.sum(jnp.where(lane == owner, w, 0.0), axis=1, keepdims=True)
            splat[row, s] = jnp.broadcast_to(chosen, (SLOTS, N))

    def sum_unit(u):
        t = lax.rem(u, SLOTS)
        mine = [splat[0, s, pl.ds(t, 1)] for s in range(RING)]
        theirs = [splat[1, s, pl.ds(t, 1)] for s in range(RING)]

        @pl.loop(0, N // 16)
        def _(i):
            rows = pl.ds(pl.multiple_of(i * 16, 16), 16)
            for s in range(RING):
                x = blocks[s, u, rows].astype(F32)
                if s == 0:
                    a, b = x * mine[s], x * theirs[s]
                else:
                    a, b = a + x * mine[s], b + x * theirs[s]
            own_sum[u, rows] = a
            away_sum[u, rows] = b

    def sum_raw(k):
        u = SUMMED + k
        t = lax.rem(u, SLOTS)
        mine = [splat[0, s, pl.ds(t, 1)] for s in range(RING)]
        theirs = [splat[2, s, pl.ds(t, 1)] for s in range(RING)]

        @pl.loop(0, N // 16)
        def _(i):
            rows = pl.ds(pl.multiple_of(i * 16, 16), 16)
            for s in range(RING):
                x, y = blocks[s, u, rows].astype(F32), blocks[s, UNITS + k, rows].astype(F32)
                if s == 0:
                    a = x * mine[s] + y * theirs[s]
                else:
                    a = a + (x * mine[s] + y * theirs[s])
            own_sum[u, rows] = a

    def place(u, total):
        c, t = u // SLOTS, lax.rem(u, SLOTS)
        first[c, t, pl.ds(TOP, N)] = total.T * root[t, pl.ds(TOP, N)]

    def unpack(field, c):
        @pl.loop(0, SLOTS)
        def _(t):
            field[t, pl.ds(TOP - 8, 8)] = strips[c][0, links[t, 0]]
            field[t, pl.ds(TOP + N, 8)] = strips[c][1, links[t, 1]]

    def read_tables():
        for copy in table_copies():
            copy.wait()
        def local(index):
            return jnp.where(index < 0, ZERO, lax.rem(jnp.maximum(index, 0), SLOTS))

        @pl.loop(0, SLOTS)
        def _(t):
            w, e = (lax.rem(jnp.maximum(neighbours[t, k], 0), SLOTS) for k in (0, 1))
            links[t, 0] = w
            links[t, 1] = e
            for k in (2, 3):
                links[t, k] = local(neighbours[t, k])
                for side, slot, back, at in ((0, w, 1, 2), (1, e, 0, 4)):
                    beyond = tables[side, slot, k]
                    via = tables[side, lax.rem(jnp.maximum(beyond, 0), SLOTS), back]
                    links[t, at + k] = jnp.where(beyond < 0, ZERO, local(via))

    lane16 = lax.broadcasted_iota(jnp.int32, (16, N), 1)

    def around(field, t, r, size, south, north):
        lanes = lane16[:size]
        y = field[t, pl.ds(r, size)]
        to_north = pltpu.roll(jnp.where(lanes == 0, field[north, pl.ds(r, size)], y), N - 1, 1)
        to_south = pltpu.roll(jnp.where(lanes == N - 1, field[south, pl.ds(r, size)], y), 1, 1)
        return (field[t, pl.ds(r + 1, size)] + field[t, pl.ds(r - 1, size)]) + (to_north + to_south)

    def pieces(t, with_strips, part=None):
        inner = range(TOP + 16, TOP + N - 16, 16)
        if with_strips and part != 0:
            yield TOP - 8, 8, links[t, 4], links[t, 5]
        for r in range(TOP, TOP + N, 16):
            if part is None or (r in inner) == (part == 0):
                yield r, 16, links[t, 2], links[t, 3]
        if with_strips and part != 0:
            yield TOP + N, 8, links[t, 6], links[t, 7]

    def prepare_gains():
        for copy in strip_copies(root, TRACERS):
            copy.wait()
        read_tables()
        unpack(root, TRACERS)

    def set_gains(t):
        results = []
        for r, size, south, north in pieces(t, True):
            side = root[t, pl.ds(r, size)]
            results.append((r, size, 1.0 - side * around(root, t, r, size, south, north), side * side))
        for r, size, kept, gained in results:
            keep[t, pl.ds(r, size)] = kept
            gain[t, pl.ds(r, size)] = gained

    def sweep(source, target, c, with_strips, part=None):
        here, there = source.at[c], target.at[c]

        @pl.loop(0, SLOTS, unroll=2)
        def _(t):
            results = []
            for r, size, south, north in pieces(t, with_strips, part):
                rows = pl.ds(r, size)
                value = keep[t, rows] * here[t, rows] + gain[t, rows] * around(
                    here, t, r, size, south, north
                )
                results.append((rows, value))
            for rows, value in results:
                there[t, rows] = value

    def begin(c):
        for copy in strip_copies(first.at[c], c):
            copy.start()

    def arrived(c):
        for copy in strip_copies(first.at[c], c):
            copy.wait()
        unpack(first.at[c], c)

    def finish(c):
        here = first.at[c]

        @pl.loop(0, SLOTS, unroll=4)
        def _(t):
            rows = pl.ds(TOP, N)
            out[t, c] = (here[t, rows] * inverse[t]).T.astype(jnp.bfloat16)

    def step(s):
        for d in (3, 2, 1):
            v = s - LAGS[d - 1]

            @pl.when(jnp.logical_and(v >= 0, v < TRAVEL))
            def _():
                ring(v, d).wait_recv()
                if d < 3:
                    ring(v, d + 1).start()
                else:

                    @pl.when(lax.rem(v, 2) == 0)
                    def _():
                        ring_far_right(v).start()

                ring(v, RING - d).wait_recv()
                if d < 3:
                    ring(v, RING - d - 1).start()
                else:

                    @pl.when(lax.rem(v, 2) == 1)
                    def _():
                        ring_far_left(v).start()

            for g, at in ((0, 0), (1, UNITS)):

                @pl.when(v == at)
                def _():
                    ring_w(g, d).wait_recv()
                    ring_w(g, d + 1).start()
                    ring_w(g, RING - d).wait_recv()
                    if d < 3:
                        ring_w(g, RING - d - 1).start()

        @pl.when(s == UNITS)
        def _():
            cross_w().wait_recv()
            ring_w(1, 1).start()
            ring_w(1, RING - 1).start()

        @pl.when(jnp.logical_and(s >= UNITS, s < TRAVEL))
        def _():
            cross_raw(s - UNITS).wait_recv()

        @pl.when(s < TRAVEL)
        def _():
            send_own(s)

        v = s - LAST

        @pl.when(v == 0)
        def _():
            ring_w(0, 4).wait_recv()
            set_splat(0, 0, member)
            set_splat(0, 1, partner)

        @pl.when(v == UNITS)
        def _():
            ring_w(1, 4).wait_recv()
            set_splat(1, 2, member)

        @pl.when(jnp.logical_and(v >= 0, v < TRAVEL))
        def _():
            ring_far_right(v).wait_recv()

        @pl.when(jnp.logical_and(v >= 0, v < SUMMED))
        def _():
            sum_unit(v)
            cross_sum(v).start()

        @pl.when(jnp.logical_and(v >= UNITS, v < TRAVEL))
        def _():
            k = v - UNITS
            sum_raw(k)
            place(SUMMED + k, own_sum[SUMMED + k])

        u = v - Y_LAG

        @pl.when(jnp.logical_and(u >= 0, u < SUMMED))
        def _():
            cross_sum(u).wait_recv()
            place(u, own_sum[u] + here_sum[u])

        @pl.when(s == LAST + 1)
        def _():
            prepare_gains()

        @pl.when(jnp.logical_and(s >= LAST + 2, s < LAST + 2 + SLOTS))
        def _():
            set_gains(s - (LAST + 2))

        @pl.when(u == SLOTS - 1)
        def _():
            begin(0)

    pl.loop(2, STEPS)(step)

    begin(1)

    arrived(0)
    sweep(first, second, 0, True)
    sweep(second, first, 0, True)
    sweep(first, second, 0, True)
    sweep(second, first, 0, False)
    finish(0)

    @pl.loop(0, TRAVEL)
    def _(v):
        for slot in (1, 2, 3, 5, 6, 7):
            ring(v, slot).wait_send()
        ring_far_right(v).wait_send()

    for g in range(2):
        for slot in range(1, RING):
            ring_w(g, slot).wait_send()
    cross_w().wait_send()

    @pl.loop(0, SUMMED)
    def _(u):
        cross_sum(u).wait_send()

    for k in range(RAW):
        cross_raw(k).wait_send()

    sweep(first, second, 1, True, 0)
    arrived(1)
    sweep(first, second, 1, True, 1)
    sweep(second, first, 1, True)
    sweep(first, second, 1, True)
    sweep(second, first, 1, False)
    finish(1)


def shards(anomalies, weights, diffusivity, land_mask, neighbours):
    anywhere = pl.BlockSpec(memory_space=pl.ANY)
    vmem = pl.BlockSpec(memory_space=pltpu.VMEM)
    result = pl.pallas_call(
        kernel,
        out_shape=jax.ShapeDtypeStruct((SLOTS, TRACERS, N, N), jnp.bfloat16),
        in_specs=[anywhere] * 5,
        out_specs=vmem,
        scratch_shapes=[
            pltpu.VMEM((RING, TRAVEL, N, N), jnp.bfloat16),
            pltpu.VMEM((2, RING, 16, N), jnp.bfloat16),
            pltpu.VMEM((3, RING, SLOTS, N), F32),
            pltpu.VMEM((UNITS, N, N), F32),
            pltpu.VMEM((SUMMED, N, N), F32),
            pltpu.VMEM((SUMMED, N, N), F32),
            pltpu.VMEM((TRACERS, SLOTS + 1, PAD, N), F32),
            pltpu.VMEM((TRACERS, SLOTS + 1, PAD, N), F32),
            pltpu.VMEM((SLOTS + 1, PAD, N), F32),
            pltpu.VMEM((SLOTS, PAD, N), F32),
            pltpu.VMEM((SLOTS, PAD, N), F32),
            pltpu.VMEM((SLOTS, N, N), F32),
            pltpu.VMEM((SLOTS, N, N), F32),
            pltpu.VMEM((SLOTS, N, N), jnp.int32),
            pltpu.VMEM((2, SLOTS, 8, N), F32),
            pltpu.VMEM((2, SLOTS, 8, N), F32),
            pltpu.VMEM((2, SLOTS, 8, N), F32),
            pltpu.SMEM((2, SLOTS, 4), jnp.int32),
            pltpu.SMEM((SLOTS, 8), jnp.int32),
            pltpu.SMEM((SLOTS, 4), jnp.int32),
            pltpu.VMEM((SLOTS, 16), jnp.bfloat16),
            pltpu.SemaphoreType.DMA((TRAVEL * RING,)),
            pltpu.SemaphoreType.DMA((TRAVEL * RING,)),
            pltpu.SemaphoreType.DMA((2 * RING,)),
            pltpu.SemaphoreType.DMA((2 * RING,)),
            pltpu.SemaphoreType.DMA((TRAVEL,)),
            pltpu.SemaphoreType.DMA((TRAVEL,)),
            pltpu.SemaphoreType.DMA((2 * TRACERS + 2,)),
            pltpu.SemaphoreType.DMA((2 * TRACERS + 2,)),
            pltpu.SemaphoreType.DMA((2,)),
            pltpu.SemaphoreType.DMA((2,)),
            pltpu.SemaphoreType.DMA((TRACERS + 4,)),
        ],
        compiler_params=pltpu.CompilerParams(
            collective_id=0, has_side_effects=True, vmem_limit_bytes=48 << 20
        ),
    )(anomalies[0], weights[0], diffusivity, land_mask, neighbours)
    return result[None]


def solution(mesh):
    return jax.shard_map(
        shards,
        mesh=mesh,
        in_specs=(
            P("member", "tile", None, None, None),
            P("member", "tile", None),
            P("tile", None, None),
            P("tile", None, None),
            P("tile", None),
        ),
        out_specs=P("member", "tile", None, None, None),
        check_vma=False,
    )
```

```python
import functools

import jax
import jax.numpy as jnp
from jax import lax
from jax.experimental import pallas as pl
from jax.experimental.pallas import tpu as pltpu
from jax.sharding import PartitionSpec as P

MESH = pl.DeviceIdType.MESH
F32 = jnp.float32

RATE = 0.2
SLOTS = 8
N = 128
TRACERS = 2
UNITS = TRACERS * SLOTS
RAW = 3
SUMMED = UNITS - RAW
TRAVEL = UNITS + RAW
RING = 8
LAGS = (2, 4, 6, 8)
Y_LAG = 6
LAST = LAGS[3]
STEPS = max(TRAVEL + LAST, SUMMED + LAST + Y_LAG)
TOP = 16
PAD = 160
ZERO = SLOTS


def kernel(
    anomalies,
    weights,
    diffusivity,
    land_mask,
    neighbour_table,
    out,
    blocks,
    own_w,
    splat,
    own_sum,
    away_sum,
    here_sum,
    first,
    second,
    root,
    keep,
    gain,
    inverse,
    diff_in,
    mask_in,
    strips_0,
    strips_1,
    strips_root,
    tables,
    links,
    neighbours,
    weights_in,
    z_send,
    z_recv,
    w_send,
    w_recv,
    y_send,
    y_recv,
    s_send,
    s_recv,
    t_send,
    t_recv,
    load,
):
    member = lax.axis_index("member")
    tile = lax.axis_index("tile")
    strips = (strips_0, strips_1, strips_root)
    half, z = member // RING, lax.rem(member, RING)
    partner = lax.rem(member + RING, 2 * RING)
    up = (half * RING + lax.rem(z + 1, RING), tile)
    down = (half * RING + lax.rem(z + RING - 1, RING), tile)
    across = (partner, tile)
    tile_devices = lax.axis_size("tile")
    before = lax.rem(tile + tile_devices - 1, tile_devices)
    behind = lax.rem(tile + 1, tile_devices)
    west, east = (member, before), (member, behind)

    def remote(src, dst, send, recv, device):
        return pltpu.make_async_remote_copy(
            src_ref=src,
            dst_ref=dst,
            send_sem=send,
            recv_sem=recv,
            device_id=device,
            device_id_type=MESH,
        )

    barrier = pltpu.get_barrier_semaphore()
    for device in (up, down, across, west, east):
        pl.semaphore_signal(barrier, inc=1, device_id=device, device_id_type=MESH)

    loads = [
        pltpu.make_async_copy(weights, weights_in, load.at[0]),
        pltpu.make_async_copy(neighbour_table, neighbours, load.at[1]),
        pltpu.make_async_copy(diffusivity, diff_in, load.at[2]),
        pltpu.make_async_copy(land_mask, mask_in, load.at[3]),
    ]
    for c in range(TRACERS):
        loads.append(
            pltpu.make_async_copy(
                anomalies.at[:, c], blocks.at[0, pl.ds(c * SLOTS, SLOTS)], load.at[4 + c]
            )
        )
    for copy in loads:
        copy.start()
    pl.semaphore_wait(barrier, 5)

    def ring(v, slot):
        rightward = slot < RING // 2
        return remote(
            blocks.at[slot - 1 if rightward else (slot + 1) % RING, v],
            blocks.at[slot, v],
            z_send.at[v * RING + slot],
            z_recv.at[v * RING + slot],
            up if rightward else down,
        )

    def ring_far_right(v):
        return remote(
            blocks.at[3, v], blocks.at[4, v], z_send.at[v * RING + 4], z_recv.at[v * RING + 4], up
        )

    def ring_far_left(v):
        return remote(
            blocks.at[5, v], blocks.at[4, v], z_send.at[v * RING + 4], z_recv.at[v * RING + 4], down
        )

    def ring_w(g, slot):
        rightward = slot <= RING // 2
        return remote(
            own_w.at[g, slot - 1 if rightward else (slot + 1) % RING],
            own_w.at[g, slot],
            w_send.at[g * RING + slot],
            w_recv.at[g * RING + slot],
            up if rightward else down,
        )

    def cross_raw(k):
        return remote(
            anomalies.at[SUMMED + k - SLOTS, 1], blocks.at[0, UNITS + k], y_send.at[UNITS + k], y_recv.at[UNITS + k], across
        )

    def cross_w():
        return remote(own_w.at[0, 0], own_w.at[1, 0], w_send.at[RING], w_recv.at[RING], across)

    def cross_sum(u):
        return remote(away_sum.at[u], here_sum.at[u], y_send.at[u], y_recv.at[u], across)

    def strip_copies(field, c):
        return (
            remote(
                field.at[pl.ds(0, SLOTS), pl.ds(TOP, 8)], strips[c].at[1], s_send.at[c * 2], s_recv.at[c * 2], west
            ),
            remote(
                field.at[pl.ds(0, SLOTS), pl.ds(TOP + N - 8, 8)],
                strips[c].at[0],
                s_send.at[c * 2 + 1],
                s_recv.at[c * 2 + 1],
                east,
            ),
        )

    def table_copies():
        return (
            remote(neighbours, tables.at[1], t_send.at[0], t_recv.at[0], west),
            remote(neighbours, tables.at[0], t_send.at[1], t_recv.at[1], east),
        )

    def send_own(s):
        ring(s, 1).start()
        ring(s, RING - 1).start()

    def send_first(v):
        for slot, device in ((1, up), (RING - 1, down)):
            remote(
                anomalies.at[v, 0], blocks.at[slot, v], z_send.at[v * RING + slot], z_recv.at[v * RING + slot], device
            ).start()

    send_first(0)
    send_first(1)
    for k in range(RAW):
        cross_raw(k).start()

    loads[0].wait()
    spread = (
        lax.broadcasted_iota(jnp.int32, (16, N), 0)
        == lax.broadcasted_iota(jnp.int32, (16, N), 1)
    ).astype(jnp.bfloat16)
    padded = jnp.dot(weights_in[...], spread, preferred_element_type=F32)
    own_w[0, 0] = jnp.concatenate([padded, jnp.zeros_like(padded)], axis=0).astype(
        jnp.bfloat16
    )
    ring_w(0, 1).start()
    ring_w(0, RING - 1).start()
    cross_w().start()
    loads[1].wait()
    for copy in table_copies():
        copy.start()
    for copy in loads[2:]:
        copy.wait()

    root[ZERO] = jnp.zeros((PAD, N), F32)
    for field in (first, second):
        for c in range(TRACERS):
            field[c, ZERO] = jnp.zeros((PAD, N), F32)

    @pl.loop(0, SLOTS)
    def _(t):
        coefficient = diff_in[t] * mask_in[t].astype(F32)
        side = jnp.sqrt(RATE * coefficient).T
        root[t, pl.ds(TOP, N)] = side
        wet = side > 0
        inverse[t] = jnp.where(wet, 1.0 / jnp.where(wet, side, 1.0), 0.0)

    for copy in strip_copies(root, TRACERS):
        copy.start()

    lane = lax.broadcasted_iota(jnp.int32, (8, N), 1)

    def set_splat(g, row, owner):
        for s in range(RING):
            w = own_w[g, s].astype(F32)[:SLOTS]
            chosen = jnp.sum(jnp.where(lane == owner, w, 0.0), axis=1, keepdims=True)
            splat[row, s] = jnp.broadcast_to(chosen, (SLOTS, N))

    def sum_unit(u):
        t = lax.rem(u, SLOTS)
        mine = [splat[0, s, pl.ds(t, 1)] for s in range(RING)]
        theirs = [splat[1, s, pl.ds(t, 1)] for s in range(RING)]

        @pl.loop(0, N // 16)
        def _(i):
            rows = pl.ds(pl.multiple_of(i * 16, 16), 16)
            for s in range(RING):
                x = blocks[s, u, rows].astype(F32)
                if s == 0:
                    a, b = x * mine[s], x * theirs[s]
                else:
                    a, b = a + x * mine[s], b + x * theirs[s]
            own_sum[u, rows] = a
            away_sum[u, rows] = b

    def sum_raw(k):
        u = SUMMED + k
        t = lax.rem(u, SLOTS)
        mine = [splat[0, s, pl.ds(t, 1)] for s in range(RING)]
        theirs = [splat[2, s, pl.ds(t, 1)] for s in range(RING)]

        @pl.loop(0, N // 16)
        def _(i):
            rows = pl.ds(pl.multiple_of(i * 16, 16), 16)
            for s in range(RING):
                x, y = blocks[s, u, rows].astype(F32), blocks[s, UNITS + k, rows].astype(F32)
                if s == 0:
                    a = x * mine[s] + y * theirs[s]
                else:
                    a = a + (x * mine[s] + y * theirs[s])
            own_sum[u, rows] = a

    def place(u, total):
        c, t = u // SLOTS, lax.rem(u, SLOTS)
        first[c, t, pl.ds(TOP, N)] = total.T * root[t, pl.ds(TOP, N)]

    def unpack(field, c):
        @pl.loop(0, SLOTS)
        def _(t):
            field[t, pl.ds(TOP - 8, 8)] = strips[c][0, links[t, 0]]
            field[t, pl.ds(TOP + N, 8)] = strips[c][1, links[t, 1]]

    def read_tables():
        for copy in table_copies():
            copy.wait()
        def local(index):
            return jnp.where(index < 0, ZERO, lax.rem(jnp.maximum(index, 0), SLOTS))

        @pl.loop(0, SLOTS)
        def _(t):
            w, e = (lax.rem(jnp.maximum(neighbours[t, k], 0), SLOTS) for k in (0, 1))
            links[t, 0] = w
            links[t, 1] = e
            for k in (2, 3):
                links[t, k] = local(neighbours[t, k])
                for side, slot, back, at in ((0, w, 1, 2), (1, e, 0, 4)):
                    beyond = tables[side, slot, k]
                    via = tables[side, lax.rem(jnp.maximum(beyond, 0), SLOTS), back]
                    links[t, at + k] = jnp.where(beyond < 0, ZERO, local(via))

    lane16 = lax.broadcasted_iota(jnp.int32, (16, N), 1)

    def around(field, t, r, size, south, north):
        lanes = lane16[:size]
        y = field[t, pl.ds(r, size)]
        to_north = pltpu.roll(jnp.where(lanes == 0, field[north, pl.ds(r, size)], y), N - 1, 1)
        to_south = pltpu.roll(jnp.where(lanes == N - 1, field[south, pl.ds(r, size)], y), 1, 1)
        return (field[t, pl.ds(r + 1, size)] + field[t, pl.ds(r - 1, size)]) + (to_north + to_south)

    def pieces(t, with_strips, part=None):
        inner = range(TOP + 16, TOP + N - 16, 16)
        if with_strips and part != 0:
            yield TOP - 8, 8, links[t, 4], links[t, 5]
        for r in range(TOP, TOP + N, 16):
            if part is None or (r in inner) == (part == 0):
                yield r, 16, links[t, 2], links[t, 3]
        if with_strips and part != 0:
            yield TOP + N, 8, links[t, 6], links[t, 7]

    def prepare_gains():
        for copy in strip_copies(root, TRACERS):
            copy.wait()
        read_tables()
        unpack(root, TRACERS)

    def set_gains(t):
        results = []
        for r, size, south, north in pieces(t, True):
            side = root[t, pl.ds(r, size)]
            results.append((r, size, 1.0 - side * around(root, t, r, size, south, north), side * side))
        for r, size, kept, gained in results:
            keep[t, pl.ds(r, size)] = kept
            gain[t, pl.ds(r, size)] = gained

    def sweep(source, target, c, with_strips, part=None):
        here, there = source.at[c], target.at[c]

        @pl.loop(0, SLOTS, unroll=4)
        def _(t):
            results = []
            for r, size, south, north in pieces(t, with_strips, part):
                rows = pl.ds(r, size)
                value = keep[t, rows] * here[t, rows] + gain[t, rows] * around(
                    here, t, r, size, south, north
                )
                results.append((rows, value))
            for rows, value in results:
                there[t, rows] = value

    def begin(c):
        for copy in strip_copies(first.at[c], c):
            copy.start()

    def arrived(c):
        for copy in strip_copies(first.at[c], c):
            copy.wait()
        unpack(first.at[c], c)

    def finish(c):
        here = first.at[c]

        @pl.loop(0, SLOTS, unroll=4)
        def _(t):
            rows = pl.ds(TOP, N)
            out[t, c] = (here[t, rows] * inverse[t]).T.astype(jnp.bfloat16)

    def step(s):
        for d in (3, 2, 1):
            v = s - LAGS[d - 1]

            @pl.when(jnp.logical_and(v >= 0, v < TRAVEL))
            def _():
                ring(v, d).wait_recv()
                if d < 3:
                    ring(v, d + 1).start()
                else:

                    @pl.when(lax.rem(v, 2) == 0)
                    def _():
                        ring_far_right(v).start()

                ring(v, RING - d).wait_recv()
                if d < 3:
                    ring(v, RING - d - 1).start()
                else:

                    @pl.when(lax.rem(v, 2) == 1)
                    def _():
                        ring_far_left(v).start()

            for g, at in ((0, 0), (1, UNITS)):

                @pl.when(v == at)
                def _():
                    ring_w(g, d).wait_recv()
                    ring_w(g, d + 1).start()
                    ring_w(g, RING - d).wait_recv()
                    if d < 3:
                        ring_w(g, RING - d - 1).start()

        @pl.when(s == UNITS)
        def _():
            cross_w().wait_recv()
            ring_w(1, 1).start()
            ring_w(1, RING - 1).start()

        @pl.when(jnp.logical_and(s >= UNITS, s < TRAVEL))
        def _():
            cross_raw(s - UNITS).wait_recv()

        @pl.when(s < TRAVEL)
        def _():
            send_own(s)

        v = s - LAST

        @pl.when(v == 0)
        def _():
            ring_w(0, 4).wait_recv()
            set_splat(0, 0, member)
            set_splat(0, 1, partner)

        @pl.when(v == UNITS)
        def _():
            ring_w(1, 4).wait_recv()
            set_splat(1, 2, member)

        @pl.when(jnp.logical_and(v >= 0, v < TRAVEL))
        def _():
            ring_far_right(v).wait_recv()

        @pl.when(jnp.logical_and(v >= 0, v < SUMMED))
        def _():
            sum_unit(v)
            cross_sum(v).start()

        @pl.when(jnp.logical_and(v >= UNITS, v < TRAVEL))
        def _():
            k = v - UNITS
            sum_raw(k)
            place(SUMMED + k, own_sum[SUMMED + k])

        u = v - Y_LAG

        @pl.when(jnp.logical_and(u >= 0, u < SUMMED))
        def _():
            cross_sum(u).wait_recv()
            place(u, own_sum[u] + here_sum[u])

        @pl.when(s == LAST + 1)
        def _():
            prepare_gains()

        @pl.when(jnp.logical_and(s >= LAST + 2, s < LAST + 2 + SLOTS))
        def _():
            set_gains(s - (LAST + 2))

        @pl.when(u == SLOTS - 1)
        def _():
            begin(0)

    pl.loop(2, STEPS)(step)

    begin(1)

    arrived(0)
    sweep(first, second, 0, True)
    sweep(second, first, 0, True)
    sweep(first, second, 0, True)
    sweep(second, first, 0, False)
    finish(0)

    @pl.loop(0, TRAVEL)
    def _(v):
        for slot in (1, 2, 3, 5, 6, 7):
            ring(v, slot).wait_send()
        ring_far_right(v).wait_send()

    for g in range(2):
        for slot in range(1, RING):
            ring_w(g, slot).wait_send()
    cross_w().wait_send()

    @pl.loop(0, SUMMED)
    def _(u):
        cross_sum(u).wait_send()

    for k in range(RAW):
        cross_raw(k).wait_send()

    sweep(first, second, 1, True, 0)
    arrived(1)
    sweep(first, second, 1, True, 1)
    sweep(second, first, 1, True)
    sweep(first, second, 1, True)
    sweep(second, first, 1, False)
    finish(1)


def shards(anomalies, weights, diffusivity, land_mask, neighbours):
    anywhere = pl.BlockSpec(memory_space=pl.ANY)
    vmem = pl.BlockSpec(memory_space=pltpu.VMEM)
    result = pl.pallas_call(
        kernel,
        out_shape=jax.ShapeDtypeStruct((SLOTS, TRACERS, N, N), jnp.bfloat16),
        in_specs=[anywhere] * 5,
        out_specs=vmem,
        scratch_shapes=[
            pltpu.VMEM((RING, TRAVEL, N, N), jnp.bfloat16),
            pltpu.VMEM((2, RING, 16, N), jnp.bfloat16),
            pltpu.VMEM((3, RING, SLOTS, N), F32),
            pltpu.VMEM((UNITS, N, N), F32),
            pltpu.VMEM((SUMMED, N, N), F32),
            pltpu.VMEM((SUMMED, N, N), F32),
            pltpu.VMEM((TRACERS, SLOTS + 1, PAD, N), F32),
            pltpu.VMEM((TRACERS, SLOTS + 1, PAD, N), F32),
            pltpu.VMEM((SLOTS + 1, PAD, N), F32),
            pltpu.VMEM((SLOTS, PAD, N), F32),
            pltpu.VMEM((SLOTS, PAD, N), F32),
            pltpu.VMEM((SLOTS, N, N), F32),
            pltpu.VMEM((SLOTS, N, N), F32),
            pltpu.VMEM((SLOTS, N, N), jnp.int32),
            pltpu.VMEM((2, SLOTS, 8, N), F32),
            pltpu.VMEM((2, SLOTS, 8, N), F32),
            pltpu.VMEM((2, SLOTS, 8, N), F32),
            pltpu.SMEM((2, SLOTS, 4), jnp.int32),
            pltpu.SMEM((SLOTS, 8), jnp.int32),
            pltpu.SMEM((SLOTS, 4), jnp.int32),
            pltpu.VMEM((SLOTS, 16), jnp.bfloat16),
            pltpu.SemaphoreType.DMA((TRAVEL * RING,)),
            pltpu.SemaphoreType.DMA((TRAVEL * RING,)),
            pltpu.SemaphoreType.DMA((2 * RING,)),
            pltpu.SemaphoreType.DMA((2 * RING,)),
            pltpu.SemaphoreType.DMA((TRAVEL,)),
            pltpu.SemaphoreType.DMA((TRAVEL,)),
            pltpu.SemaphoreType.DMA((2 * TRACERS + 2,)),
            pltpu.SemaphoreType.DMA((2 * TRACERS + 2,)),
            pltpu.SemaphoreType.DMA((2,)),
            pltpu.SemaphoreType.DMA((2,)),
            pltpu.SemaphoreType.DMA((TRACERS + 4,)),
        ],
        compiler_params=pltpu.CompilerParams(
            collective_id=0, has_side_effects=True, vmem_limit_bytes=48 << 20
        ),
    )(anomalies[0], weights[0], diffusivity, land_mask, neighbours)
    return result[None]


def solution(mesh):
    return jax.shard_map(
        shards,
        mesh=mesh,
        in_specs=(
            P("member", "tile", None, None, None),
            P("member", "tile", None),
            P("tile", None, None),
            P("tile", None, None),
            P("tile", None),
        ),
        out_specs=P("member", "tile", None, None, None),
        check_vma=False,
    )
```
